512 devices in a mesh: dp: 64 (over z_lo, x, y), tensor: 8 (over z_hi, core).
Axes of the slice: x: 4, y: 8, z: 8 (z_hi: 4, z_lo: 2; z = z_hi * 2 + z_lo), core: 2. Of those that a mesh axis runs over, the one named last changes fastest.
Arguments:
- grad_part: bfloat16 [64, 4, 192, 5120], P('dp', None, None, 'tensor'), may hold values from -16 to 16
- hess_part: bfloat16 [64, 4, 192, 5120], P('dp', None, None, 'tensor'), may hold values from 0.5 to 5
- momentum: float32 [4, 192, 5120], P(None, 'dp', 'tensor'), may hold values from -18 to 18
- hessian: float32 [4, 192, 5120], P(None, 'dp', 'tensor'), may hold values from 0.2 to 2
- master: float32 [4, 192, 5120], P(None, 'dp', 'tensor'), may hold values from -0.078125 to 0.078125
- step: int32 [1], replicated, may hold values from 1 to 100
- refresh: int32 [4], replicated, may hold values from 0 to 1, as said below
Outputs:
- new_momentum: float32 [4, 192, 5120], P(None, 'dp', 'tensor')
- new_hessian: float32 [4, 192, 5120], P(None, 'dp', 'tensor')
- new_master: float32 [4, 192, 5120], P(None, 'dp', 'tensor')
- weights: bfloat16 [4, 192, 5120], P(None, None, 'tensor')
- clip_fraction: float32 [1], replicated
The draws below stay inside these ranges and needn't reach their ends.
Inputs may be any that keep to these rules, and one draw needn't show every extreme that they name: `refresh`: each flag is 0 or 1; at least one layer has 1 and at least one has 0.
All inputs are finite; a program needn't handle non-finite values.
Results may differ from the reference program's by a relative error of at most 0.001.
Values may be sent and summed in bfloat16 or wider, within the bound.
No kernel may reach another device: no remote copies, remote signals or barrier semaphores. Data moves between devices by JAX's collectives and lax.ppermute only.
A program may use at most 64 MiB of HBM per device.

```python
import math
import jax
import jax.numpy as jnp

D = 5120
LAYERS = 4
LROWS = 192
N_DP = 64


def draw_momentum(key, part):
    key = jax.random.fold_in(key, 3)
    row_frac = jnp.arange(LROWS, dtype=jnp.float32) / LROWS
    values = jnp.clip(jax.random.normal(key, (LAYERS, LROWS, D), jnp.float32), -6.0, 6.0)
    row_scale = jnp.exp(jnp.log(0.3) + jnp.log(10.0) * row_frac)
    return values * row_scale[None, :, None]


def draw_refresh(key, part):
    key = jax.random.fold_in(key, 5)
    key_bits, key_on, key_off = jax.random.split(key, 3)
    layer_flags = jax.random.randint(key_bits, (LAYERS,), 0, 2)
    chosen = jax.random.randint(key_on, (), 0, LAYERS)
    unused = (chosen + 1 + jax.random.randint(key_off, (), 0, LAYERS - 1)) % LAYERS
    positions = jnp.arange(LAYERS)
    layer_flags = jnp.where(positions == chosen, 1, jnp.where(positions == unused, 0, layer_flags))
    return layer_flags.astype(jnp.int32)


def with_spikes(entries, key, source, target, blocks, factor):
    owner, partner = [(jnp.arange(entries.shape[position]) // (entries.shape[position] // blocks)).reshape([-1 if axis == position else 1 for axis in range(entries.ndim)]) for position in (source, target)]
    chosen = jax.random.permutation(key, blocks)[partner]
    strong = (owner == chosen) | (owner == (partner + blocks // 2) % blocks)
    return jnp.where(strong, factor * entries, entries)


def block_scale(rng, shape, shards, least, top_value):
    def one(axis_at, blocks):
        steps = jax.random.uniform(jax.random.fold_in(jax.random.fold_in(rng, 6), axis_at), (blocks,), jnp.float32, least / len(shards), top_value / len(shards))
        return jnp.repeat(jnp.exp(steps), shape[axis_at] // blocks).reshape((-1,) + (1,) * (len(shape) - axis_at - 1))

    loudness = one(*shards[0])
    for cut in shards[1:]:
        loudness = loudness * one(*cut)
    return loudness


def centred(stream_key, dims, width, limit, shards=(), kind=jnp.bfloat16):
    drawn = width * jax.random.normal(stream_key, dims, jnp.float32)
    if shards:
        drawn = drawn * block_scale(stream_key, dims, shards, -0.22, 0.18)
    return jnp.clip(drawn, -limit, limit).astype(kind)


def gaussian_with(stream_key, dims, spread, limit, cuts, heavy, held_as=jnp.bfloat16):
    values = spread * jax.random.normal(stream_key, dims, jnp.float32)
    if cuts:
        values = values * block_scale(stream_key, dims, cuts, -0.22, 0.18)
    return jnp.clip(with_spikes(values, jax.random.fold_in(stream_key, 3), *heavy), -limit, limit).astype(held_as)


def setup_inputs(seed: int = 0) -> dict:
    splits = jax.random.split(jax.random.key(seed), 8)
    return {
        "grad_part": gaussian_with(splits[0], (N_DP, LAYERS, LROWS, D), 1.0, 16.0, ((0, 64), (3, 8)), (0, 2, 64, 4.0)),
        "hess_part": jnp.clip(jnp.exp(math.log(5.0) - 2.3025851 * jax.random.uniform(splits[1], (N_DP, LAYERS, LROWS, D), jnp.float32) ** block_scale(splits[1], (N_DP, LAYERS, LROWS, D), ((0, 64), (3, 8)), -0.2, 0.2)), 0.5, 5.0).astype(jnp.bfloat16),
        "momentum": draw_momentum(jax.random.fold_in(splits[7], 71), 0),
        "hessian": jnp.clip(jnp.exp(math.log(2.0) - 2.3025851 * jax.random.uniform(splits[3], (LAYERS, LROWS, D), jnp.float32) ** block_scale(splits[3], (LAYERS, LROWS, D), ((1, 64), (2, 8)), -0.2, 0.2)), 0.2, 2.0),
        "master": centred(splits[4], (LAYERS, LROWS, D), D ** -0.5, 0.078125, ((1, 64), (2, 8)), jnp.float32),
        "step": jax.random.randint(splits[5], (1,), 1, 101).astype(jnp.int32),
        "refresh": draw_refresh(jax.random.fold_in(splits[7], 71), 0),
    }


BETA_ONE = 0.965
BETA_TWO = 0.99
RHO_SCALE = 0.5
LEARN_RATE = 0.0006
DECAY_RATE = 0.1


def reference(grad_part, hess_part, momentum, hessian, master, step, refresh):
    grad_sum = jnp.sum(grad_part, axis=0, dtype=jnp.float32)
    hess_sum = jnp.sum(hess_part, axis=0, dtype=jnp.float32)
    new_momentum = BETA_ONE * momentum + (1.0 - BETA_ONE) * grad_sum
    layer_flags = (refresh > 0)[:, None, None]
    new_hessian = jnp.where(layer_flags, BETA_TWO * hessian + (1.0 - BETA_TWO) * hess_sum, hessian)
    correction = 1.0 - jnp.power(jnp.float32(BETA_ONE), step[0].astype(jnp.float32))
    ratios = (new_momentum / correction) / (RHO_SCALE * new_hessian)
    clipped = jnp.clip(ratios, -1.0, 1.0)
    new_master = master * (1.0 - LEARN_RATE * DECAY_RATE) - LEARN_RATE * clipped
    weights = new_master.astype(jnp.bfloat16)
    clipped_count = jnp.sum((jnp.abs(ratios) >= 1.0).astype(jnp.float32))
    clip_fraction = jnp.reshape(clipped_count / ratios.size, (1,))
    return new_momentum, new_hessian, new_master, weights, clip_fraction
```

```python
import jax
import jax.numpy as jnp
from jax import lax
from jax.sharding import Mesh
from jax.sharding import PartitionSpec as P

BETA_ONE = 0.965
BETA_TWO = 0.99
RHO_SCALE = 0.5
LEARN_RATE = 0.0006
DECAY_RATE = 0.1

ZL, X, Y, ZH, CORE = 2, 4, 8, 4, 2
DP = ("zl", "x", "y")
TENSOR = ("zh", "core")
FIRST = ("zl", "x")
BASE = 256.0


def exchange(blocks, axes):
    return lax.all_to_all(blocks, axes, split_axis=0, concat_axis=0, tiled=False)


def digits(count):
    high = jnp.floor(count * (1.0 / BASE))
    return high, count - BASE * high


def local(grad_part, hess_part, momentum, hessian, master, step, refresh):
    layers, rows, cols = grad_part.shape[1:]
    outer, inner = ZL * X, Y
    block, own = rows // outer, rows // (outer * inner)

    flags = (refresh > 0).astype(jnp.int32)
    place = jnp.cumsum(flags) - flags
    slots = layers - 1
    picks = [
        jnp.sum(jnp.where((flags > 0) & (place == s), jnp.arange(layers), 0)) for s in range(slots)
    ]
    hess_used = [lax.dynamic_index_in_dim(hess_part[0], p, 0, keepdims=True) for p in picks]
    stacked = jnp.concatenate([grad_part[0]] + hess_used, axis=0)
    lots = layers + slots
    blocks = stacked.reshape(lots, outer, block, cols).transpose(1, 0, 2, 3)

    came = exchange(blocks, FIRST)
    partial = jnp.sum(came.astype(jnp.float32), axis=0)
    partial = partial.reshape(lots, inner, own, cols).transpose(1, 0, 2, 3)
    came = exchange(partial.reshape(inner, lots * own, cols), "y")
    sums = jnp.sum(came, axis=0).reshape(lots, own, cols)
    grad_sum = sums[:layers]
    hess_sum = jnp.stack(
        [
            lax.dynamic_index_in_dim(sums, layers + jnp.minimum(place[l], slots - 1), 0, keepdims=False)
            for l in range(layers)
        ]
    )

    new_momentum = BETA_ONE * momentum + (1.0 - BETA_ONE) * grad_sum
    layer_flags = (refresh > 0)[:, None, None]
    new_hessian = jnp.where(layer_flags, BETA_TWO * hessian + (1.0 - BETA_TWO) * hess_sum, hessian)
    correction = 1.0 - jnp.power(jnp.float32(BETA_ONE), step[0].astype(jnp.float32))
    ratios = new_momentum / correction / (RHO_SCALE * new_hessian)
    clipped = jnp.clip(ratios, -1.0, 1.0)
    new_master = master * (1.0 - LEARN_RATE * DECAY_RATE) - LEARN_RATE * clipped
    mine = new_master.astype(jnp.bfloat16)
    count = jnp.sum((jnp.abs(ratios) >= 1.0).astype(jnp.float32))

    high, low = digits(count)
    tail = jnp.stack([high, low, high, low]).astype(jnp.bfloat16)
    tail = jnp.broadcast_to(tail[:, None], (4, cols))
    load = jnp.concatenate([mine.reshape(layers * own, cols), tail], axis=0)
    came = exchange(jnp.broadcast_to(load[None], (inner,) + load.shape), "y")
    held = came[:, : layers * own].reshape(inner, layers, own, cols).transpose(1, 0, 2, 3)
    held = held.reshape(layers * block, cols)
    marks = came[:, layers * own : layers * own + 2, 0].astype(jnp.float32)
    count = jnp.sum(marks[:, 0] * BASE + marks[:, 1])

    high, low = digits(count)
    tail = jnp.stack([high, low] * 8).astype(jnp.bfloat16)
    tail = jnp.broadcast_to(tail[:, None], (16, cols))
    load = jnp.concatenate([held, tail], axis=0)
    came = exchange(jnp.broadcast_to(load[None], (outer,) + load.shape), FIRST)
    weights = came[:, : layers * block].reshape(outer, layers, block, cols).transpose(1, 0, 2, 3)
    weights = weights.reshape(layers, rows, cols)
    marks = came[:, layers * block : layers * block + 2, 0].astype(jnp.float32)
    count = jnp.sum(marks[:, 0] * BASE + marks[:, 1])

    came = exchange(jnp.broadcast_to(count, (ZH * CORE, 1, 128)), TENSOR)
    total = jnp.sum(came[:, 0, 0])
    entries = ratios.size * outer * inner * ZH * CORE
    clip_fraction = jnp.reshape(total / entries, (1,))
    return (new_momentum, new_hessian, new_master, weights, clip_fraction)


def solution(mesh):
    fine = Mesh(mesh.devices.reshape(ZL, X, Y, ZH, CORE), DP + TENSOR)
    shards = P(DP, None, None, TENSOR)
    state = P(None, DP, TENSOR)
    in_specs = (shards, shards, state, state, state, P(), P())
    out_specs = (state, state, state, P(None, None, TENSOR), P())
    return jax.shard_map(local, mesh=fine, in_specs=in_specs, out_specs=out_specs, check_vma=False)
```

```python
import jax
import jax.numpy as jnp
from jax import lax
from jax.sharding import Mesh
from jax.sharding import PartitionSpec as P

BETA_ONE = 0.965
BETA_TWO = 0.99
RHO_SCALE = 0.5
LEARN_RATE = 0.0006
DECAY_RATE = 0.1

ZL, X, Y, ZH, CORE = 2, 4, 8, 4, 2
DP = ("zl", "x", "y")
TENSOR = ("zh", "core")
FIRST = ("zl", "x")
LIFT = 256.0


def exchange(blocks, axes):
    return lax.all_to_all(blocks, axes, split_axis=0, concat_axis=0, tiled=False)


def encode(v):
    w = v * LIFT
    w2 = w * w
    w4 = w2 * w2
    w8 = w4 * w4
    return jnp.where(v < 0.0, -w8, w8).astype(jnp.bfloat16)


def decode(code):
    t = code.astype(jnp.float32)
    size = jnp.sqrt(jnp.sqrt(jnp.sqrt(jnp.abs(t)))) * (1.0 / LIFT)
    return jnp.where(t < 0.0, -size, size)


def local(grad_part, hess_part, momentum, hessian, master, step, refresh):
    layers, rows, cols = grad_part.shape[1:]
    outer, inner = ZL * X, Y
    block, own = rows // outer, rows // (outer * inner)
    slots = layers - 1
    lots = layers + slots

    idle = [jnp.reshape(refresh[l : l + 1] <= 0, (1, 1, 1)) for l in range(layers)]
    past = [idle[0]]
    for l in range(1, slots):
        past.append(past[-1] | idle[l])
    grad, hess = grad_part[0], hess_part[0]
    chosen = [jnp.where(past[s], hess[s + 1 : s + 2], hess[s : s + 1]) for s in range(slots)]
    stacked = jnp.concatenate([grad] + chosen, axis=0)
    blocks = stacked.reshape(lots, outer, block, cols).transpose(1, 0, 2, 3)

    came = exchange(blocks, FIRST)
    partial = jnp.sum(came.astype(jnp.float32), axis=0)
    partial = partial.reshape(lots, inner, own, cols).transpose(1, 0, 2, 3)
    came = exchange(encode(partial).reshape(inner, lots * own, cols), "y")
    sums = jnp.sum(decode(came), axis=0).reshape(lots, own, cols)
    grad_sum = sums[:layers]
    held = [sums[layers + s : layers + s + 1] for s in range(slots)]
    hess_sum = jnp.concatenate(
        [held[0]]
        + [jnp.where(past[l - 1], held[l - 1], held[l]) for l in range(1, slots)]
        + [held[slots - 1]],
        axis=0,
    )

    new_momentum = BETA_ONE * momentum + (1.0 - BETA_ONE) * grad_sum
    layer_flags = (refresh > 0)[:, None, None]
    new_hessian = jnp.where(layer_flags, BETA_TWO * hessian + (1.0 - BETA_TWO) * hess_sum, hessian)
    correction = 1.0 - jnp.power(jnp.float32(BETA_ONE), step.astype(jnp.float32))
    ratios = new_momentum / jnp.reshape(correction, (1, 1, 1)) / (RHO_SCALE * new_hessian)
    clipped = jnp.clip(ratios, -1.0, 1.0)
    new_master = master * (1.0 - LEARN_RATE * DECAY_RATE) - LEARN_RATE * clipped
    mine = new_master.astype(jnp.bfloat16)
    count = jnp.sum((jnp.abs(ratios) >= 1.0).astype(jnp.float32), axis=(0, 1))[None]

    load = jnp.concatenate([mine.reshape(layers * own, cols), count.astype(jnp.bfloat16)], axis=0)
    load = jnp.pad(load, ((0, 3), (0, 0)))
    came = exchange(jnp.broadcast_to(load[None], (inner,) + load.shape), "y")
    held = came[:, : layers * own].reshape(inner, layers, own, cols).transpose(1, 0, 2, 3)
    held = held.reshape(layers * block, cols)
    count = jnp.sum(came[:, layers * own].astype(jnp.float32), axis=0)[None]

    load = jnp.concatenate([held, count.astype(jnp.bfloat16)], axis=0)
    load = jnp.pad(load, ((0, 15), (0, 0)))
    came = exchange(jnp.broadcast_to(load[None], (outer,) + load.shape), FIRST)
    weights = came[:, : layers * block].reshape(outer, layers, block, cols).transpose(1, 0, 2, 3)
    weights = weights.reshape(layers, rows, cols)
    count = jnp.sum(came[:, layers * block].astype(jnp.float32), axis=0)

    count = jnp.sum(count.reshape(cols // 128, 128), axis=0)
    came = exchange(jnp.broadcast_to(count[None, None], (ZH * CORE, 1, 128)), TENSOR)
    total = jnp.sum(came)
    entries = ratios.size * outer * inner * ZH * CORE
    clip_fraction = jnp.reshape(total / entries, (1,))
    return (new_momentum, new_hessian, new_master, weights, clip_fraction)


def solution(mesh):
    fine = Mesh(mesh.devices.reshape(ZL, X, Y, ZH, CORE), DP + TENSOR)
    shards = P(DP, None, None, TENSOR)
    state = P(None, DP, TENSOR)
    in_specs = (shards, shards, state, state, state, P(), P())
    out_specs = (state, state, state, P(None, None, TENSOR), P())
    return jax.shard_map(local, mesh=fine, in_specs=in_specs, out_specs=out_specs, check_vma=False)
```

```python
import jax
import jax.numpy as jnp
from jax import lax
from jax.experimental import pallas as pl
from jax.experimental.pallas import tpu as pltpu
from jax.sharding import Mesh
from jax.sharding import PartitionSpec as P

BETA_ONE = 0.965
BETA_TWO = 0.99
RHO_SCALE = 0.5
LEARN_RATE = 0.0006
DECAY_RATE = 0.1

ZL, X, Y, ZH, CORE = 2, 4, 8, 4, 2
DP = ("zl", "x", "y")
TENSOR = ("zh", "core")
FIRST = ("zl", "x")
LIFT = 256.0


def exchange(blocks, axes):
    return lax.all_to_all(blocks, axes, split_axis=0, concat_axis=0, tiled=False)


def encode(v):
    w = v * LIFT
    w2 = w * w
    w4 = w2 * w2
    w8 = w4 * w4
    return jnp.where(v < 0.0, -w8, w8).astype(jnp.bfloat16)


def decode(code):
    t = code.astype(jnp.float32)
    size = jnp.sqrt(jnp.sqrt(jnp.sqrt(jnp.abs(t)))) * (1.0 / LIFT)
    return jnp.where(t < 0.0, -size, size)


def pack_kernel(refresh, grad, hess, blocks, flags, flag_sem, sems):
    layers = grad.shape[0]
    read = pltpu.make_async_copy(refresh, flags, flag_sem)
    read.start()
    copies = [pltpu.make_async_copy(grad.at[l], blocks.at[:, l], sems.at[l]) for l in range(layers)]
    for copy in copies:
        copy.start()
    read.wait()
    past = jnp.int32(0)
    for s in range(layers - 1):
        past = jnp.where(flags[s] > 0, past, 1)
        copy = pltpu.make_async_copy(hess.at[s + past], blocks.at[:, layers + s], sems.at[layers + s])
        copy.start()
        copies.append(copy)
    for copy in copies:
        copy.wait()


def pack(refresh, grad, hess):
    layers, outer, block, cols = grad.shape
    lots = 2 * layers - 1
    return pl.pallas_call(
        pack_kernel,
        out_shape=pltpu.VMEM((outer, lots, block, cols), grad.dtype),
        in_specs=[pl.BlockSpec(memory_space=pl.ANY)] * 3,
        out_specs=pl.BlockSpec(memory_space=pl.ANY),
        scratch_shapes=[
            pltpu.SMEM((layers,), jnp.int32),
            pltpu.SemaphoreType.DMA,
            pltpu.SemaphoreType.DMA((lots,)),
        ],
        compiler_params=pltpu.CompilerParams(vmem_limit_bytes=8 * 1024 * 1024),
        name="pack",
    )(*(pltpu.with_memory_space_constraint(a, pltpu.HBM) for a in (refresh, grad, hess)))


def local(grad_part, hess_part, momentum, hessian, master, step, refresh):
    layers, rows, cols = grad_part.shape[1:]
    outer, inner = ZL * X, Y
    block, own = rows // outer, rows // (outer * inner)
    slots = layers - 1
    lots = layers + slots

    idle = [jnp.reshape(refresh[l : l + 1] <= 0, (1, 1, 1)) for l in range(layers)]
    past = [idle[0]]
    for l in range(1, slots):
        past.append(past[-1] | idle[l])
    shape = (layers, outer, block, cols)
    blocks = pack(refresh, grad_part.reshape(shape), hess_part.reshape(shape))

    came = exchange(blocks, FIRST)
    partial = jnp.sum(came.astype(jnp.float32), axis=0)
    partial = partial.reshape(lots, inner, own, cols).transpose(1, 0, 2, 3)
    came = exchange(encode(partial).reshape(inner, lots * own, cols), "y")
    sums = jnp.sum(decode(came), axis=0).reshape(lots, own, cols)
    grad_sum = sums[:layers]
    held = [sums[layers + s : layers + s + 1] for s in range(slots)]
    hess_sum = jnp.concatenate(
        [held[0]]
        + [jnp.where(past[l - 1], held[l - 1], held[l]) for l in range(1, slots)]
        + [held[slots - 1]],
        axis=0,
    )

    new_momentum = BETA_ONE * momentum + (1.0 - BETA_ONE) * grad_sum
    layer_flags = (refresh > 0)[:, None, None]
    new_hessian = jnp.where(layer_flags, BETA_TWO * hessian + (1.0 - BETA_TWO) * hess_sum, hessian)
    correction = 1.0 - jnp.power(jnp.float32(BETA_ONE), step.astype(jnp.float32))
    ratios = new_momentum / jnp.reshape(correction, (1, 1, 1)) / (RHO_SCALE * new_hessian)
    clipped = jnp.clip(ratios, -1.0, 1.0)
    new_master = master * (1.0 - LEARN_RATE * DECAY_RATE) - LEARN_RATE * clipped
    mine = new_master.astype(jnp.bfloat16)
    count = jnp.sum((jnp.abs(ratios) >= 1.0).astype(jnp.float32), axis=(0, 1))[None]

    load = jnp.concatenate([mine.reshape(layers * own, cols), count.astype(jnp.bfloat16)], axis=0)
    load = jnp.pad(load, ((0, 3), (0, 0)))
    came = exchange(jnp.broadcast_to(load[None], (inner,) + load.shape), "y")
    held = came[:, : layers * own].reshape(inner, layers, own, cols).transpose(1, 0, 2, 3)
    held = held.reshape(layers * block, cols)
    count = jnp.sum(came[:, layers * own].astype(jnp.float32), axis=0)[None]

    load = jnp.concatenate([held, count.astype(jnp.bfloat16)], axis=0)
    came = exchange(jnp.broadcast_to(load[None], (outer,) + load.shape), FIRST)
    weights = came[:, : layers * block].reshape(outer, layers, block, cols).transpose(1, 0, 2, 3)
    weights = weights.reshape(layers, rows, cols)
    count = jnp.sum(came[:, layers * block].astype(jnp.float32), axis=0)

    count = jnp.sum(count.reshape(cols // 128, 128), axis=0)
    came = exchange(jnp.broadcast_to(count[None, None], (ZH * CORE, 1, 128)), TENSOR)
    total = jnp.sum(came)
    entries = ratios.size * outer * inner * ZH * CORE
    clip_fraction = jnp.reshape(total / entries, (1,))
    return (new_momentum, new_hessian, new_master, weights, clip_fraction)


def solution(mesh):
    fine = Mesh(mesh.devices.reshape(ZL, X, Y, ZH, CORE), DP + TENSOR)
    shards = P(DP, None, None, TENSOR)
    state = P(None, DP, TENSOR)
    in_specs = (shards, shards, state, state, state, P(), P())
    out_specs = (state, state, state, P(None, None, TENSOR), P())
    return jax.shard_map(local, mesh=fine, in_specs=in_specs, out_specs=out_specs, check_vma=False)
```

```python
import functools

import jax
import jax.numpy as jnp
from jax import lax
from jax.experimental import pallas as pl
from jax.experimental.pallas import tpu as pltpu
from jax.sharding import Mesh
from jax.sharding import PartitionSpec as P

BETA_ONE = 0.965
BETA_TWO = 0.99
RHO_SCALE = 0.5
LEARN_RATE = 0.0006
DECAY_RATE = 0.1

ZL, X, Y, ZH, CORE = 2, 4, 8, 4, 2
DP = ("zl", "x", "y")
TENSOR = ("zh", "core")
FIRST = ("zl", "x")
LIFT = 256.0


def exchange(blocks, axes):
    return lax.all_to_all(blocks, axes, split_axis=0, concat_axis=0, tiled=False)


def encode(v):
    w = v * LIFT
    w2 = w * w
    w4 = w2 * w2
    w8 = w4 * w4
    return jnp.where(v < 0.0, -w8, w8)


def decode(code):
    t = code.astype(jnp.float32)
    size = jnp.sqrt(jnp.sqrt(jnp.sqrt(jnp.abs(t)))) * (1.0 / LIFT)
    return jnp.where(t < 0.0, -size, size)


def pack_kernel(slots, refresh, grad, hess, blocks, marks, flags, flag_sem, sems):
    layers = grad.shape[0]
    read = pltpu.make_async_copy(refresh, flags, flag_sem)
    read.start()
    copies = [pltpu.make_async_copy(grad.at[l], blocks.at[:, l], sems.at[l]) for l in range(layers)]
    for copy in copies:
        copy.start()
    read.wait()
    ranks, rank = [], jnp.int32(0)
    picks = [jnp.int32(0)] * slots
    for l in range(layers):
        used = flags[l] > 0
        picks = [jnp.where(used & (rank == s), l, picks[s]) for s in range(slots)]
        ranks.append(rank)
        rank = rank + used.astype(jnp.int32)
    for s in range(slots):
        copy = pltpu.make_async_copy(hess.at[picks[s]], blocks.at[:, layers + s], sems.at[layers + s])
        copy.start()
        copies.append(copy)
    for l in range(layers):
        flag = (flags[l] > 0).astype(jnp.float32)
        marks[l : l + 1] = jnp.full((1, marks.shape[1]), ranks[l].astype(jnp.float32))
        marks[layers + l : layers + l + 1] = jnp.full((1, marks.shape[1]), flag)
    for copy in copies:
        copy.wait()


def pack(slots, refresh, grad, hess):
    layers, outer, block, cols = grad.shape
    lots = layers + slots
    return pl.pallas_call(
        functools.partial(pack_kernel, slots),
        out_shape=(
            pltpu.VMEM((outer, lots, block, cols), grad.dtype),
            pltpu.VMEM((2 * layers, cols), jnp.float32),
        ),
        in_specs=[pl.BlockSpec(memory_space=pl.ANY)] * 3,
        out_specs=(pl.BlockSpec(memory_space=pl.ANY), pl.BlockSpec(memory_space=pltpu.VMEM)),
        scratch_shapes=[
            pltpu.SMEM((layers,), jnp.int32),
            pltpu.SemaphoreType.DMA,
            pltpu.SemaphoreType.DMA((lots,)),
        ],
        compiler_params=pltpu.CompilerParams(vmem_limit_bytes=8 * 1024 * 1024),
        name="pack",
    )(*(pltpu.with_memory_space_constraint(a, pltpu.HBM) for a in (refresh, grad, hess)))


def fold_kernel(own, came, codes, rows):
    outer, lots, block, _ = came.shape
    for lot in range(lots):
        total = came[0, lot].astype(jnp.float32)
        for k in range(1, outer):
            total += came[k, lot].astype(jnp.float32)
        code = encode(total)
        for y in range(block // own):
            rows[y, lot * own : (lot + 1) * own] = code[y * own : (y + 1) * own]
    codes[...] = rows[...].astype(codes.dtype)


def fold(came):
    _, lots, block, cols = came.shape
    own = block // Y
    shape = (Y, lots * own, cols)
    return pl.pallas_call(
        functools.partial(fold_kernel, own),
        out_shape=pltpu.VMEM(shape, came.dtype),
        in_specs=[pl.BlockSpec(memory_space=pltpu.VMEM)],
        out_specs=pl.BlockSpec(memory_space=pltpu.VMEM),
        scratch_shapes=[pltpu.VMEM(shape, jnp.float32)],
        compiler_params=pltpu.CompilerParams(vmem_limit_bytes=16 * 1024 * 1024),
        name="fold",
    )(pltpu.with_memory_space_constraint(came, pltpu.VMEM))


def reduce(slots, grad_part, hess_part, refresh):
    layers, rows, cols = grad_part.shape[1:]
    outer, inner = ZL * X, Y
    block, own = rows // outer, rows // (outer * inner)
    shape = (layers, outer, block, cols)
    blocks, marks = pack(slots, refresh, grad_part.reshape(shape), hess_part.reshape(shape))
    came = exchange(fold(exchange(blocks, FIRST)), "y")
    sums = jnp.sum(decode(came), axis=0)
    parts = [sums[: layers * own]]
    held = [sums[(layers + s) * own : (layers + s + 1) * own] for s in range(slots)]
    for l in range(layers):
        mine = held[0]
        for s in range(1, min(l + 1, slots)):
            mine = jnp.where(marks[l : l + 1] >= s, held[s], mine)
        parts.append(mine)
    return jnp.concatenate(parts + [marks[layers:]], axis=0)


def branch_kernel(refresh, index, flags, sem):
    read = pltpu.make_async_copy(refresh, flags, sem)
    read.start()
    read.wait()
    layers = refresh.shape[0]
    count = jnp.int32(0)
    for l in range(layers):
        count = count + (flags[l] > 0).astype(jnp.int32)
    index[0] = jnp.clip(count, 1, layers - 1) - 1


def branch(refresh):
    return pl.pallas_call(
        branch_kernel,
        out_shape=pltpu.SMEM((1,), jnp.int32),
        in_specs=[pl.BlockSpec(memory_space=pl.ANY)],
        out_specs=pl.BlockSpec(memory_space=pltpu.SMEM),
        scratch_shapes=[pltpu.SMEM(refresh.shape, jnp.int32), pltpu.SemaphoreType.DMA],
        compiler_params=pltpu.CompilerParams(vmem_limit_bytes=1024 * 1024),
        name="branch",
    )(pltpu.with_memory_space_constraint(refresh, pltpu.HBM))[0]


def local(grad_part, hess_part, momentum, hessian, master, step, refresh):
    layers, rows, cols = grad_part.shape[1:]
    outer, inner = ZL * X, Y
    block, own = rows // outer, rows // (outer * inner)

    sums = lax.switch(
        branch(refresh),
        [functools.partial(reduce, slots) for slots in range(1, layers)],
        grad_part,
        hess_part,
        refresh,
    )
    grad_sum = sums[: layers * own].reshape(layers, own, cols)
    hess_sum = sums[layers * own : 2 * layers * own].reshape(layers, own, cols)
    layer_flags = sums[2 * layers * own :][:, None, :] > 0.0

    new_momentum = BETA_ONE * momentum + (1.0 - BETA_ONE) * grad_sum
    new_hessian = jnp.where(layer_flags, BETA_TWO * hessian + (1.0 - BETA_TWO) * hess_sum, hessian)
    correction = 1.0 - jnp.power(jnp.float32(BETA_ONE), step.astype(jnp.float32))
    ratios = new_momentum / jnp.reshape(correction, (1, 1, 1)) / (RHO_SCALE * new_hessian)
    clipped = jnp.clip(ratios, -1.0, 1.0)
    new_master = master * (1.0 - LEARN_RATE * DECAY_RATE) - LEARN_RATE * clipped
    mine = new_master.astype(jnp.bfloat16)
    count = jnp.sum((jnp.abs(ratios) >= 1.0).astype(jnp.float32), axis=(0, 1))[None]

    load = jnp.concatenate([mine.reshape(layers * own, cols), count.astype(jnp.bfloat16)], axis=0)
    load = jnp.pad(load, ((0, 3), (0, 0)))
    came = exchange(jnp.broadcast_to(load[None], (inner,) + load.shape), "y")
    held = came[:, : layers * own].reshape(inner, layers, own, cols).transpose(1, 0, 2, 3)
    held = held.reshape(layers * block, cols)
    count = jnp.sum(came[:, layers * own].astype(jnp.float32), axis=0)[None]

    load = jnp.concatenate([held, count.astype(jnp.bfloat16)], axis=0)
    came = exchange(jnp.broadcast_to(load[None], (outer,) + load.shape), FIRST)
    weights = came[:, : layers * block].reshape(outer, layers, block, cols).transpose(1, 0, 2, 3)
    weights = weights.reshape(layers, rows, cols)
    count = jnp.sum(came[:, layers * block].astype(jnp.float32), axis=0)

    count = jnp.sum(count.reshape(cols // 128, 128), axis=0)
    came = exchange(jnp.broadcast_to(count[None, None], (ZH * CORE, 1, 128)), TENSOR)
    total = jnp.sum(came)
    entries = layers * rows * cols * ZH * CORE
    clip_fraction = jnp.reshape(total / entries, (1,))
    return (new_momentum, new_hessian, new_master, weights, clip_fraction)


def solution(mesh):
    fine = Mesh(mesh.devices.reshape(ZL, X, Y, ZH, CORE), DP + TENSOR)
    shards = P(DP, None, None, TENSOR)
    state = P(None, DP, TENSOR)
    in_specs = (shards, shards, state, state, state, P(), P())
    out_specs = (state, state, state, P(None, None, TENSOR), P())
    return jax.shard_map(local, mesh=fine, in_specs=in_specs, out_specs=out_specs, check_vma=False)
```

```python
import functools

import jax
import jax.numpy as jnp
from jax import lax
from jax.experimental import pallas as pl
from jax.experimental.pallas import tpu as pltpu
from jax.sharding import Mesh
from jax.sharding import PartitionSpec as P

BETA_ONE = 0.965
BETA_TWO = 0.99
RHO_SCALE = 0.5
LEARN_RATE = 0.0006
DECAY_RATE = 0.1

ZL, X, Y, ZH, CORE = 2, 4, 8, 4, 2
DP = ("zl", "x", "y")
TENSOR = ("zh", "core")
FIRST = ("zl", "x")
LIFT = 256.0


def exchange(blocks, axes):
    return lax.all_to_all(blocks, axes, split_axis=0, concat_axis=0, tiled=False)


def encode(v):
    w = v * LIFT
    w2 = w * w
    w4 = w2 * w2
    w8 = w4 * w4
    return jnp.where(v < 0.0, -w8, w8)


def decode(code):
    t = code.astype(jnp.float32)
    size = jnp.sqrt(jnp.sqrt(jnp.sqrt(jnp.abs(t)))) * (1.0 / LIFT)
    return jnp.where(t < 0.0, -size, size)


def pack_kernel(slots, refresh, grad, hess, blocks, marks, flags, flag_sem, sems):
    layers = grad.shape[0]
    read = pltpu.make_async_copy(refresh, flags, flag_sem)
    read.start()
    copies = [pltpu.make_async_copy(grad.at[l], blocks.at[:, l], sems.at[l]) for l in range(layers)]
    for copy in copies:
        copy.start()
    read.wait()
    ranks, rank = [], jnp.int32(0)
    picks = [jnp.int32(0)] * slots
    for l in range(layers):
        used = flags[l] > 0
        picks = [jnp.where(used & (rank == s), l, picks[s]) for s in range(slots)]
        ranks.append(rank)
        rank = rank + used.astype(jnp.int32)
    for s in range(slots):
        copy = pltpu.make_async_copy(hess.at[picks[s]], blocks.at[:, layers + s], sems.at[layers + s])
        copy.start()
        copies.append(copy)
    for l in range(layers):
        flag = (flags[l] > 0).astype(jnp.float32)
        marks[l : l + 1] = jnp.full((1, marks.shape[1]), ranks[l].astype(jnp.float32))
        marks[layers + l : layers + l + 1] = jnp.full((1, marks.shape[1]), flag)
    for copy in copies:
        copy.wait()


def pack(slots, refresh, grad, hess):
    layers, outer, block, cols = grad.shape
    lots = layers + slots
    return pl.pallas_call(
        functools.partial(pack_kernel, slots),
        out_shape=(
            pltpu.VMEM((outer, lots, block, cols), grad.dtype),
            pltpu.VMEM((2 * layers, cols), jnp.float32),
        ),
        in_specs=[pl.BlockSpec(memory_space=pl.ANY)] * 3,
        out_specs=(pl.BlockSpec(memory_space=pl.ANY), pl.BlockSpec(memory_space=pltpu.VMEM)),
        scratch_shapes=[
            pltpu.SMEM((layers,), jnp.int32),
            pltpu.SemaphoreType.DMA,
            pltpu.SemaphoreType.DMA((lots,)),
        ],
        compiler_params=pltpu.CompilerParams(vmem_limit_bytes=8 * 1024 * 1024),
        name="pack",
    )(*(pltpu.with_memory_space_constraint(a, pltpu.HBM) for a in (refresh, grad, hess)))


def fold_kernel(own, came, codes, rows):
    outer, lots, block, cols = came.shape
    for lot in range(lots):
        for col in range(0, cols, 128):
            lanes = slice(col, col + 128)
            terms = [came[k, lot, :, lanes].astype(jnp.float32) for k in range(outer)]
            while len(terms) > 1:
                terms = [a + b for a, b in zip(terms[::2], terms[1::2])]
            code = encode(terms[0])
            for y in range(block // own):
                rows[y, lot * own : (lot + 1) * own, lanes] = code[y * own : (y + 1) * own]
    codes[...] = rows[...].astype(codes.dtype)


def fold(came):
    _, lots, block, cols = came.shape
    own = block // Y
    shape = (Y, lots * own, cols)
    return pl.pallas_call(
        functools.partial(fold_kernel, own),
        out_shape=pltpu.VMEM(shape, came.dtype),
        in_specs=[pl.BlockSpec(memory_space=pltpu.VMEM)],
        out_specs=pl.BlockSpec(memory_space=pltpu.VMEM),
        scratch_shapes=[pltpu.VMEM(shape, jnp.float32)],
        compiler_params=pltpu.CompilerParams(vmem_limit_bytes=16 * 1024 * 1024),
        name="fold",
    )(pltpu.with_memory_space_constraint(came, pltpu.VMEM))


def reduce(slots, grad_part, hess_part, refresh):
    layers, rows, cols = grad_part.shape[1:]
    outer, inner = ZL * X, Y
    block, own = rows // outer, rows // (outer * inner)
    shape = (layers, outer, block, cols)
    blocks, marks = pack(slots, refresh, grad_part.reshape(shape), hess_part.reshape(shape))
    came, marks = lax.optimization_barrier((exchange(fold(exchange(blocks, FIRST)), "y"), marks))
    sums = jnp.sum(decode(came), axis=0)
    parts = [sums[: layers * own]]
    held = [sums[(layers + s) * own : (layers + s + 1) * own] for s in range(slots)]
    for l in range(layers):
        mine = held[0]
        for s in range(1, min(l + 1, slots)):
            mine = jnp.where(marks[l : l + 1] >= s, held[s], mine)
        parts.append(mine)
    return jnp.concatenate(parts + [marks[layers:]], axis=0)


def branch_kernel(refresh, index, flags, sem):
    read = pltpu.make_async_copy(refresh, flags, sem)
    read.start()
    read.wait()
    layers = refresh.shape[0]
    count = jnp.int32(0)
    for l in range(layers):
        count = count + (flags[l] > 0).astype(jnp.int32)
    index[0] = jnp.clip(count, 1, layers - 1) - 1


def branch(refresh):
    return pl.pallas_call(
        branch_kernel,
        out_shape=pltpu.SMEM((1,), jnp.int32),
        in_specs=[pl.BlockSpec(memory_space=pl.ANY)],
        out_specs=pl.BlockSpec(memory_space=pltpu.SMEM),
        scratch_shapes=[pltpu.SMEM(refresh.shape, jnp.int32), pltpu.SemaphoreType.DMA],
        compiler_params=pltpu.CompilerParams(vmem_limit_bytes=1024 * 1024),
        name="branch",
    )(pltpu.with_memory_space_constraint(refresh, pltpu.HBM))[0]


def local(grad_part, hess_part, momentum, hessian, master, step, refresh):
    layers, rows, cols = grad_part.shape[1:]
    outer, inner = ZL * X, Y
    block, own = rows // outer, rows // (outer * inner)

    sums = lax.switch(
        branch(refresh),
        [functools.partial(reduce, slots) for slots in range(1, layers)],
        grad_part,
        hess_part,
        refresh,
    )
    grad_sum = sums[: layers * own].reshape(layers, own, cols)
    hess_sum = sums[layers * own : 2 * layers * own].reshape(layers, own, cols)
    layer_flags = sums[2 * layers * own :][:, None, :] > 0.0

    new_momentum = BETA_ONE * momentum + (1.0 - BETA_ONE) * grad_sum
    new_hessian = jnp.where(layer_flags, BETA_TWO * hessian + (1.0 - BETA_TWO) * hess_sum, hessian)
    correction = 1.0 - jnp.power(jnp.float32(BETA_ONE), step.astype(jnp.float32))
    ratios = new_momentum / jnp.reshape(correction, (1, 1, 1)) / (RHO_SCALE * new_hessian)
    clipped = jnp.clip(ratios, -1.0, 1.0)
    new_master = master * (1.0 - LEARN_RATE * DECAY_RATE) - LEARN_RATE * clipped
    mine = new_master.astype(jnp.bfloat16)
    count = jnp.sum((jnp.abs(ratios) >= 1.0).astype(jnp.float32), axis=(0, 1))[None]

    load = jnp.concatenate([mine.reshape(layers * own, cols), count.astype(jnp.bfloat16)], axis=0)
    load = jnp.pad(load, ((0, 3), (0, 0)))
    came = exchange(jnp.broadcast_to(load[None], (inner,) + load.shape), "y")
    held = came[:, : layers * own].reshape(inner, layers, own, cols).transpose(1, 0, 2, 3)
    held = held.reshape(layers * block, cols)
    count = jnp.sum(came[:, layers * own].astype(jnp.float32), axis=0)[None]

    load = jnp.concatenate([held, count.astype(jnp.bfloat16)], axis=0)
    came = exchange(jnp.broadcast_to(load[None], (outer,) + load.shape), FIRST)
    weights = came[:, : layers * block].reshape(outer, layers, block, cols).transpose(1, 0, 2, 3)
    weights = weights.reshape(layers, rows, cols)
    count = jnp.sum(came[:, layers * block].astype(jnp.float32), axis=0)

    count = jnp.sum(count.reshape(cols // 128, 128), axis=0)
    came = exchange(jnp.broadcast_to(count[None, None], (ZH * CORE, 1, 128)), TENSOR)
    total = jnp.sum(came)
    entries = layers * rows * cols * ZH * CORE
    clip_fraction = jnp.reshape(total / entries, (1,))
    return (new_momentum, new_hessian, new_master, weights, clip_fraction)


def solution(mesh):
    fine = Mesh(mesh.devices.reshape(ZL, X, Y, ZH, CORE), DP + TENSOR)
    shards = P(DP, None, None, TENSOR)
    state = P(None, DP, TENSOR)
    in_specs = (shards, shards, state, state, state, P(), P())
    out_specs = (state, state, state, P(None, None, TENSOR), P())
    return jax.shard_map(local, mesh=fine, in_specs=in_specs, out_specs=out_specs, check_vma=False)
```

```python
import functools

import jax
import jax.numpy as jnp
from jax import lax
from jax.experimental import pallas as pl
from jax.experimental.pallas import tpu as pltpu
from jax.sharding import Mesh
from jax.sharding import PartitionSpec as P

BETA_ONE = 0.965
BETA_TWO = 0.99
RHO_SCALE = 0.5
LEARN_RATE = 0.0006
DECAY_RATE = 0.1

ZL, X, Y, ZH, CORE = 2, 4, 8, 4, 2
DP = ("zl", "x", "y")
TENSOR = ("zh", "core")
FIRST = ("zl", "x")
LIFT = 256.0


def exchange(blocks, axes):
    return lax.all_to_all(blocks, axes, split_axis=0, concat_axis=0, tiled=False)


def encode(v):
    w = v * LIFT
    w2 = w * w
    w4 = w2 * w2
    w8 = w4 * w4
    return jnp.where(v < 0.0, -w8, w8)


def decode(code):
    t = code.astype(jnp.float32)
    size = jnp.sqrt(jnp.sqrt(jnp.sqrt(jnp.abs(t)))) * (1.0 / LIFT)
    return jnp.where(t < 0.0, -size, size)


def pack_kernel(slots, refresh, grad, hess, blocks, marks, flags, flag_sem, sems):
    layers = grad.shape[0]
    read = pltpu.make_async_copy(refresh, flags, flag_sem)
    read.start()
    copies = [pltpu.make_async_copy(grad.at[l], blocks.at[:, l], sems.at[l]) for l in range(layers)]
    for copy in copies:
        copy.start()
    read.wait()
    ranks, rank = [], jnp.int32(0)
    picks = [jnp.int32(0)] * slots
    for l in range(layers):
        used = flags[l] > 0
        picks = [jnp.where(used & (rank == s), l, picks[s]) for s in range(slots)]
        ranks.append(rank)
        rank = rank + used.astype(jnp.int32)
    for s in range(slots):
        copy = pltpu.make_async_copy(hess.at[picks[s]], blocks.at[:, layers + s], sems.at[layers + s])
        copy.start()
        copies.append(copy)
    for l in range(layers):
        flag = (flags[l] > 0).astype(jnp.float32)
        marks[l : l + 1] = jnp.full((1, marks.shape[1]), ranks[l].astype(jnp.float32))
        marks[layers + l : layers + l + 1] = jnp.full((1, marks.shape[1]), flag)
    for copy in copies:
        copy.wait()


def pack(slots, refresh, grad, hess):
    layers, outer, block, cols = grad.shape
    lots = layers + slots
    return pl.pallas_call(
        functools.partial(pack_kernel, slots),
        out_shape=(
            pltpu.VMEM((outer, lots, block, cols), grad.dtype),
            pltpu.VMEM((2 * layers, cols), jnp.float32),
        ),
        in_specs=[pl.BlockSpec(memory_space=pl.ANY)] * 3,
        out_specs=(pl.BlockSpec(memory_space=pl.ANY), pl.BlockSpec(memory_space=pltpu.VMEM)),
        scratch_shapes=[
            pltpu.SMEM((layers,), jnp.int32),
            pltpu.SemaphoreType.DMA,
            pltpu.SemaphoreType.DMA((lots,)),
        ],
        compiler_params=pltpu.CompilerParams(vmem_limit_bytes=8 * 1024 * 1024),
        name="pack",
    )(*(pltpu.with_memory_space_constraint(a, pltpu.HBM) for a in (refresh, grad, hess)))


def fold_kernel(own, came, codes, rows):
    outer, lots, block, cols = came.shape
    for lot in range(lots):
        for col in range(0, cols, 128):
            lanes = slice(col, col + 128)
            terms = [came[k, lot, :, lanes].astype(jnp.float32) for k in range(outer)]
            while len(terms) > 1:
                terms = [a + b for a, b in zip(terms[::2], terms[1::2])]
            code = encode(terms[0])
            for y in range(block // own):
                rows[y, lot * own : (lot + 1) * own, lanes] = code[y * own : (y + 1) * own]
    codes[...] = rows[...].astype(codes.dtype)


def fold(came):
    _, lots, block, cols = came.shape
    own = block // Y
    shape = (Y, lots * own, cols)
    return pl.pallas_call(
        functools.partial(fold_kernel, own),
        out_shape=pltpu.VMEM(shape, came.dtype),
        in_specs=[pl.BlockSpec(memory_space=pltpu.VMEM)],
        out_specs=pl.BlockSpec(memory_space=pltpu.VMEM),
        scratch_shapes=[pltpu.VMEM(shape, jnp.float32)],
        compiler_params=pltpu.CompilerParams(vmem_limit_bytes=16 * 1024 * 1024),
        name="fold",
    )(pltpu.with_memory_space_constraint(came, pltpu.VMEM))


def reduce(slots, grad_part, hess_part, refresh):
    layers, rows, cols = grad_part.shape[1:]
    outer, inner = ZL * X, Y
    block, own = rows // outer, rows // (outer * inner)
    shape = (layers, outer, block, cols)
    blocks, marks = pack(slots, refresh, grad_part.reshape(shape), hess_part.reshape(shape))
    came, marks = lax.optimization_barrier((exchange(fold(exchange(blocks, FIRST)), "y"), marks))
    sums = jnp.sum(decode(came), axis=0)
    parts = [sums[: layers * own]]
    held = [sums[(layers + s) * own : (layers + s + 1) * own] for s in range(slots)]
    for l in range(layers):
        mine = held[0]
        for s in range(1, min(l + 1, slots)):
            mine = jnp.where(marks[l : l + 1] >= s, held[s], mine)
        parts.append(mine)
    return jnp.concatenate(parts + [marks[layers:]], axis=0)


def branch_kernel(refresh, index, flags, sem):
    read = pltpu.make_async_copy(refresh, flags, sem)
    read.start()
    read.wait()
    layers = refresh.shape[0]
    count = jnp.int32(0)
    for l in range(layers):
        count = count + (flags[l] > 0).astype(jnp.int32)
    index[0] = jnp.clip(count, 1, layers - 1) - 1


def branch(refresh):
    return pl.pallas_call(
        branch_kernel,
        out_shape=pltpu.SMEM((1,), jnp.int32),
        in_specs=[pl.BlockSpec(memory_space=pl.ANY)],
        out_specs=pl.BlockSpec(memory_space=pltpu.SMEM),
        scratch_shapes=[pltpu.SMEM(refresh.shape, jnp.int32), pltpu.SemaphoreType.DMA],
        compiler_params=pltpu.CompilerParams(vmem_limit_bytes=1024 * 1024),
        name="branch",
    )(pltpu.with_memory_space_constraint(refresh, pltpu.HBM))[0]


def local(grad_part, hess_part, momentum, hessian, master, step, refresh):
    layers, rows, cols = grad_part.shape[1:]
    outer, inner = ZL * X, Y
    block, own = rows // outer, rows // (outer * inner)

    sums = lax.switch(
        branch(refresh),
        [functools.partial(reduce, slots) for slots in range(1, layers)],
        grad_part,
        hess_part,
        refresh,
    )
    grad_sum = sums[: layers * own].reshape(layers, own, cols)
    hess_sum = sums[layers * own : 2 * layers * own].reshape(layers, own, cols)
    layer_flags = sums[2 * layers * own :][:, None, :] > 0.0

    new_momentum = BETA_ONE * momentum + (1.0 - BETA_ONE) * grad_sum
    new_hessian = jnp.where(layer_flags, BETA_TWO * hessian + (1.0 - BETA_TWO) * hess_sum, hessian)
    correction = 1.0 - jnp.power(jnp.float32(BETA_ONE), step.astype(jnp.float32))
    ratios = new_momentum / jnp.reshape(correction, (1, 1, 1)) / (RHO_SCALE * new_hessian)
    clipped = jnp.clip(ratios, -1.0, 1.0)
    new_master = master * (1.0 - LEARN_RATE * DECAY_RATE) - LEARN_RATE * clipped
    mine = new_master.astype(jnp.bfloat16)
    count = jnp.sum((jnp.abs(ratios) >= 1.0).astype(jnp.float32), axis=(0, 1))[None]

    load = jnp.concatenate([mine.reshape(layers * own, cols), count.astype(jnp.bfloat16)], axis=0)
    load = jnp.pad(load, ((0, 3), (0, 0)))
    came = exchange(jnp.broadcast_to(load[None], (inner,) + load.shape), "y")
    held = came[:, : layers * own].reshape(inner, layers, own, cols).transpose(1, 0, 2, 3)
    held = held.reshape(layers * block, cols)
    count = jnp.sum(came[:, layers * own].astype(jnp.float32), axis=0)[None]

    held = held.reshape(-1, 8, cols // 128, 128).transpose(0, 2, 1, 3).reshape(-1, 128)
    load = jnp.concatenate([held, count.astype(jnp.bfloat16).reshape(-1, 128)], axis=0)
    came = exchange(jnp.broadcast_to(load[None], (outer,) + load.shape), FIRST)
    size = held.shape[0]
    weights = came[:, :size].reshape(outer, layers, block // 8, cols // 128, 8, 128)
    weights = weights.transpose(1, 0, 2, 4, 3, 5).reshape(layers, rows, cols)
    count = jnp.sum(came[:, size:].astype(jnp.float32), axis=0)

    count = jnp.sum(count, axis=0)
    came = exchange(jnp.broadcast_to(count[None, None], (ZH * CORE, 1, 128)), TENSOR)
    total = jnp.sum(came)
    entries = layers * rows * cols * ZH * CORE
    clip_fraction = jnp.reshape(total / entries, (1,))
    return (new_momentum, new_hessian, new_master, weights, clip_fraction)


def solution(mesh):
    fine = Mesh(mesh.devices.reshape(ZL, X, Y, ZH, CORE), DP + TENSOR)
    shards = P(DP, None, None, TENSOR)
    state = P(None, DP, TENSOR)
    in_specs = (shards, shards, state, state, state, P(), P())
    out_specs = (state, state, state, P(None, None, TENSOR), P())
    return jax.shard_map(local, mesh=fine, in_specs=in_specs, out_specs=out_specs, check_vma=False)
```
